32 devices in a mesh: expert: 16 (over z, y, core), replica: 2 (over x).
Axes of the slice: x: 2, y: 2, z: 4, core: 2. Of those that a mesh axis runs over, the one named last changes fastest.
Arguments:
- hidden_first: bfloat16 [256, 4096], P(('expert', 'replica')), may hold values from -40 to 40
- hidden_second: bfloat16 [256, 4096], P(('expert', 'replica')), may hold values from -40 to 40
- routes_first: int32 [256, 8], P(('expert', 'replica')), may hold values from 0 to 15, all different within a row; in each aligned block of 8 rows (0 to 7, 8 to 15, ...) at most 8 rows name the same one
- routes_second: int32 [256, 8], P(('expert', 'replica')), may hold values from 0 to 15, all different within a row; in each aligned block of 8 rows (0 to 7, 8 to 15, ...) at most 8 rows name the same one
- mixing_first: float32 [256, 8], P(('expert', 'replica')), may hold values from 0.05 to 0.5
- mixing_second: float32 [256, 8], P(('expert', 'replica')), may hold values from 0.05 to 0.5
- norm_gain: float32 [4096], replicated, may hold values from 0.1 to 1.9
- expert_owner: int32 [16], replicated, may hold values from 0 to 15, each once
- swap_flags: int32 [16], replicated, may hold values from 0 to 1, as said below
- gate_up_values: bfloat16 [16, 2, 4096, 1024], P('expert', None, None, 'replica'), may hold values from -0.09375 to 0.09375
- gate_up_scales: bfloat16 [16, 2, 32, 8], P('expert', None, None, 'replica'), may hold values from 0.5 to 2
- down_values: bfloat16 [16, 1024, 4096], P('expert', 'replica'), may hold values from -0.1875 to 0.1875
- down_scales: bfloat16 [16, 8, 32], P('expert', 'replica'), may hold values from 0.5 to 2
Outputs:
- output_first: bfloat16 [256, 4096], P(('expert', 'replica'))
- output_second: bfloat16 [256, 4096], P(('expert', 'replica'))
- gate_up_moved: bfloat16 [16, 2, 4096, 1024], P('expert', None, None, 'replica')
- gate_up_scales_moved: bfloat16 [16, 2, 32, 8], P('expert', None, None, 'replica')
- down_moved: bfloat16 [16, 1024, 4096], P('expert', 'replica')
- down_scales_moved: bfloat16 [16, 8, 32], P('expert', 'replica')
The draws below stay inside these ranges and needn't reach their ends.
Inputs may be any that keep to these rules, and one draw needn't show every extreme that they name: swap_flags[d] equals swap_flags[(d + 8) mod 16].
All inputs are finite; a program needn't handle non-finite values.
Results may differ from the reference program's by a relative error of at most 0.012.
Values may be sent and summed in bfloat16 or wider, within the bound.
A program may use at most 192 MiB of HBM per device.

```python
import math
import jax
import jax.numpy as jnp
import numpy as np
from jax import lax

D = 4096
FFW = 1024
TOPK = 8
BLOCK = 128
TOK_DEV = 8
EXPERTS = 16
CAP = 8
TOKENS = 256
N_EXPERT = 16
N_REPLICA = 2


def spread_field(key):
    base_key, row_key, col_key = jax.random.split(key, 3)
    values = jnp.clip(jax.random.normal(base_key, (TOKENS, D), jnp.float32), -4.0, 4.0)
    row_scale = jnp.exp(jax.random.uniform(row_key, (TOKENS, 1), jnp.float32, -1.15, 1.15))
    col_scale = jnp.exp(jax.random.uniform(col_key, (1, D), jnp.float32, -1.15, 1.15))
    return values * row_scale * col_scale


def draw_hidden_first(key, part):
    return spread_field(jax.random.fold_in(key, 11)).astype(jnp.bfloat16)


def draw_hidden_second(key, part):
    return spread_field(jax.random.fold_in(key, 23)).astype(jnp.bfloat16)


def draw_swap_flags(key, part):
    halfway = EXPERTS // 2
    leading = jax.random.randint(jax.random.fold_in(key, 37), (halfway,), 0, 2).astype(jnp.int32)
    leading = leading.at[0].set(1).at[1].set(0)
    return jnp.concatenate([leading, leading])


def shard_levels(rng, extent, pieces, smallest, top_value):
    gain, own = 1.0, jax.random.fold_in(rng, 6)
    for axis_at, parts in pieces:
        heights = jnp.exp(jax.random.uniform(jax.random.fold_in(own, axis_at), (parts,), jnp.float32, smallest / len(pieces), top_value / len(pieces)))
        gain = gain * jnp.repeat(heights, extent[axis_at] // parts).reshape([-1 if axis == axis_at else 1 for axis in range(len(extent))])
    return gain


def shared_out(rng, own, number, rows, count, top, most, lean):
    order = jax.random.permutation(rng, count)
    crowded, common = load_shares(count, rows * top, most, lean, True), load_shares(count, rows * top, most, lean, False)
    places = jnp.arange(count)

    def named(lengths, turn):
        used = int((lengths > 0).sum())
        fixed = max(1, used // 4)
        passed = fixed + (places - fixed + turn * (used - fixed)) % max(1, count - fixed)
        return jnp.zeros((count,), jnp.int32).at[order[jnp.where(places < fixed, places, passed)]].set(jnp.asarray(lengths, jnp.int32))

    lengths = jnp.where(number % 4 == 0, named(crowded, number // 4), named(common, number - number // 4 - 1))
    mixed = jax.random.permutation(jax.random.fold_in(own, 3), count)
    source_of, taker = mixed[0:count // 2 * 2:2], mixed[1:count // 2 * 2:2]
    margin = jnp.minimum(lengths[source_of] - 1, most - lengths[taker]) // 2
    margin = jnp.where((source_of == order[0]) | (taker == order[0]) | (lengths[taker] == 0), 0, jnp.maximum(margin, 0))
    passed = jax.random.randint(jax.random.fold_in(own, 4), (count // 2,), 0, 1 << 20) % (margin + 1)
    lengths = lengths.at[source_of].add(-passed).at[taker].add(passed)
    items = jnp.searchsorted(jnp.cumsum(lengths), jnp.arange(rows * top), side="right").astype(jnp.int32)
    table = items.reshape(top, rows).T
    table = table[jax.random.permutation(jax.random.fold_in(own, 1), rows)]
    turn = jax.random.randint(jax.random.fold_in(own, 2), (rows, 1), 0, top)
    return jnp.take_along_axis(table, (jnp.arange(top)[None, :] + turn) % top, axis=1)


def load_shares(number_of, total, most, slope, full):
    weights = [(1 << 20) // math.isqrt(standing ** slope) + 1 for standing in range(1, number_of + 1)]
    largest = most if full else min(most, max(-(-total // number_of), total * weights[0] // sum(weights)))
    least = 1 if total - largest >= number_of - 1 else 0
    counts, spare = [largest] + [least] * (number_of - 1), total - largest - least * (number_of - 1)
    while spare > 0:
        movable = [i for i in range(1, number_of) if counts[i] < largest] or [i for i in range(1, number_of) if counts[i] < most]
        pool, budget = sum([weights[i] for i in movable]), spare
        for i in movable:
            addition = min(most - counts[i], max(1, budget * weights[i] // pool), spare)
            counts[i] = counts[i] + addition
            spare = spare - addition
    return np.array(counts)


def normal_values(rng, extent, deviation, bound, cuts=(), kind=jnp.bfloat16):
    entries = deviation * jax.random.normal(rng, extent, jnp.float32)
    if cuts:
        entries = entries * shard_levels(rng, extent, cuts, -0.22, 0.18)
    return jnp.clip(entries, -bound, bound).astype(kind)


def setup_inputs(seed: int = 0) -> dict:
    splits = jax.random.split(jax.random.key(seed), 14)
    hidden_first = draw_hidden_first(jax.random.fold_in(splits[13], 71), 0)
    hidden_second = draw_hidden_second(jax.random.fold_in(splits[13], 71), 0)
    routes_first_keys = jax.random.split(jax.random.fold_in(splits[2], 1), TOKENS // TOK_DEV)
    routes_first_turns = jax.random.permutation(jax.random.fold_in(splits[2], 3), TOKENS // TOK_DEV)
    routes_first = jax.vmap(lambda own, number: shared_out(jax.random.fold_in(splits[2], 2), own, number, TOK_DEV, EXPERTS, TOPK, CAP, 2))(routes_first_keys, routes_first_turns).reshape((TOKENS, TOPK))
    routes_second_keys = jax.random.split(jax.random.fold_in(splits[3], 1), TOKENS // TOK_DEV)
    routes_second_turns = jax.random.permutation(jax.random.fold_in(splits[3], 3), TOKENS // TOK_DEV)
    routes_second = jax.vmap(lambda own, number: shared_out(jax.random.fold_in(splits[3], 2), own, number, TOK_DEV, EXPERTS, TOPK, CAP, 2))(routes_second_keys, routes_second_turns).reshape((TOKENS, TOPK))
    mixing_first = jnp.clip(jnp.exp(math.log(0.5) - 2.3025851 * jax.random.uniform(splits[4], (TOKENS, TOPK), jnp.float32) ** shard_levels(splits[4], (TOKENS, TOPK), ((0, 32),), -0.2, 0.2)), 0.05, 0.5)
    mixing_second = jnp.clip(jnp.exp(math.log(0.5) - 2.3025851 * jax.random.uniform(splits[5], (TOKENS, TOPK), jnp.float32) ** shard_levels(splits[5], (TOKENS, TOPK), ((0, 32),), -0.2, 0.2)), 0.05, 0.5)
    norm_gain = jnp.clip(1.0 + 0.18 * jax.random.normal(splits[6], (D,), jnp.float32), 0.1, 1.9)
    expert_owner = jax.random.permutation(splits[7], EXPERTS).astype(jnp.int32)
    swap_flags = draw_swap_flags(jax.random.fold_in(splits[13], 71), 0)
    gate_up_values = normal_values(splits[9], (EXPERTS, 2, D, FFW), D ** -0.5, 0.09375, ((0, 16), (3, 2)))
    gate_up_scales = jnp.clip(jnp.exp(math.log(2.0) - 1.3862944 * jax.random.uniform(splits[10], (EXPERTS, 2, D // BLOCK, FFW // BLOCK), jnp.float32) ** shard_levels(splits[10], (EXPERTS, 2, D // BLOCK, FFW // BLOCK), ((0, 16), (3, 2)), -0.2, 0.2)), 0.5, 2.0).astype(jnp.bfloat16)
    down_values = normal_values(splits[11], (EXPERTS, FFW, D), FFW ** -0.5, 0.1875, ((0, 16), (1, 2)))
    down_scales = jnp.clip(jnp.exp(math.log(2.0) - 1.3862944 * jax.random.uniform(splits[12], (EXPERTS, FFW // BLOCK, D // BLOCK), jnp.float32) ** shard_levels(splits[12], (EXPERTS, FFW // BLOCK, D // BLOCK), ((0, 16), (1, 2)), -0.2, 0.2)), 0.5, 2.0).astype(jnp.bfloat16)
    return dict(hidden_first=hidden_first, hidden_second=hidden_second, routes_first=routes_first, routes_second=routes_second, mixing_first=mixing_first, mixing_second=mixing_second, norm_gain=norm_gain, expert_owner=expert_owner, swap_flags=swap_flags, gate_up_values=gate_up_values, gate_up_scales=gate_up_scales, down_values=down_values, down_scales=down_scales)


def dequantize(values, scales):
    height, breadth = (values.shape[-2], values.shape[-1])
    block_rows, block_cols = (scales.shape[-2], scales.shape[-1])
    leading = values.shape[:-2]
    blocked = values.astype(jnp.float32).reshape(leading + (block_rows, height // block_rows, block_cols, breadth // block_cols))
    scaled = blocked * scales.astype(jnp.float32)[..., :, None, :, None]
    return scaled.reshape(values.shape).astype(jnp.bfloat16)

def rms_normed(hidden, norm_gain):
    widened = hidden.astype(jnp.float32)
    inverse_rms = lax.rsqrt(lax.optimization_barrier(jnp.mean(widened * widened, axis=-1, keepdims=True)) + 1e-06)
    return (widened * inverse_rms * norm_gain).astype(jnp.bfloat16)

def rounded(partial_sum):
    return lax.optimization_barrier(partial_sum.astype(jnp.bfloat16)).astype(jnp.float32)

def expert_output(token_rows, gate_up, down_proj):
    gate_act = jnp.dot(token_rows, gate_up[0], preferred_element_type=jnp.float32)
    up_act = jnp.dot(token_rows, gate_up[1], preferred_element_type=jnp.float32)
    inner_act = (jax.nn.silu(gate_act) * up_act).astype(jnp.bfloat16)
    share_width = down_proj.shape[0] // N_REPLICA
    running = jnp.zeros((token_rows.shape[0], down_proj.shape[1]), jnp.float32)
    for block_index in range(N_REPLICA):
        lower_edge = block_index * share_width
        partial_piece = jnp.dot(inner_act[:, lower_edge:lower_edge + share_width], down_proj[lower_edge:lower_edge + share_width], preferred_element_type=jnp.float32)
        running = running + rounded(partial_piece)
    return running.astype(jnp.bfloat16)

def layer_step(hidden, routes, mixing, norm_gain, weights_of):
    normed = rms_normed(hidden, norm_gain)
    pick_experts = routes.reshape(-1).astype(jnp.int32)
    pick_tokens = (jnp.arange(pick_experts.shape[0], dtype=jnp.int32) // TOPK).astype(jnp.int32)
    pick_weights = mixing.reshape(-1)
    row_limit = N_EXPERT * N_REPLICA * CAP

    def visit_expert(running, expert_id):
        matches = pick_experts == expert_id
        found_rows = jnp.nonzero(matches, size=row_limit, fill_value=0)[0].astype(jnp.int32)
        filled = (jnp.arange(row_limit, dtype=jnp.int32) < jnp.sum(matches.astype(jnp.int32))).astype(pick_weights.dtype)
        token_ids = pick_tokens[found_rows]
        gate_up, down_proj = weights_of(expert_id)
        result = expert_output(normed[token_ids], gate_up, down_proj).astype(pick_weights.dtype)
        shares = pick_weights[found_rows] * filled
        return (running.at[token_ids].add(result * shares[:, None]), None)
    start_sum = jnp.zeros(hidden.shape, pick_weights.dtype)
    running, _unused = lax.scan(visit_expert, start_sum, jnp.arange(EXPERTS, dtype=jnp.int32))
    return running.astype(jnp.bfloat16)

def reference(hidden_first, hidden_second, routes_first, routes_second, mixing_first, mixing_second, norm_gain, expert_owner, swap_flags, gate_up_values, gate_up_scales, down_values, down_scales):
    slot_ids = jnp.arange(EXPERTS, dtype=jnp.int32)
    source = jnp.where(swap_flags == 1, (slot_ids + EXPERTS // 2) % EXPERTS, slot_ids).astype(jnp.int32)
    moved_arrays = tuple((source_array[source] for source_array in (gate_up_values, gate_up_scales, down_values, down_scales)))

    def weights_of(expert_id):
        home_slot = expert_owner[expert_id]
        return (dequantize(gate_up_values[home_slot], gate_up_scales[home_slot]), dequantize(down_values[home_slot], down_scales[home_slot]))
    output_first = layer_step(hidden_first, routes_first, mixing_first, norm_gain, weights_of)
    output_second = layer_step(hidden_second, routes_second, mixing_second, norm_gain, weights_of)
    return (output_first, output_second, moved_arrays[0], moved_arrays[1], moved_arrays[2], moved_arrays[3])
```

```python
import functools

import jax
import jax.numpy as jnp
from jax import lax
from jax.experimental import pallas as pl
from jax.experimental.pallas import tpu as pltpu
from jax.sharding import PartitionSpec as P

LANES = 128


def partner(block, axis, bit):
    count = lax.axis_size(axis)
    route = [(low, low ^ (1 << bit)) for low in range(count)]
    return lax.ppermute(block, axis, route)


def rms_normed(hidden, norm_gain):
    widened = hidden.astype(jnp.float32)
    inverse_rms = lax.rsqrt(jnp.mean(widened * widened, axis=-1, keepdims=True) + 1e-06)
    return (widened * inverse_rms * norm_gain).astype(jnp.bfloat16)


def expert_kernel(rows_ref, gate_up_ref, gate_up_scale_ref, down_ref, down_scale_ref, share_ref, out_ref, total):
    step = pl.program_id(0)
    features = rows_ref.shape[1]
    blocks = gate_up_scale_ref.shape[2]
    height = features // blocks

    def projection(index):
        values = gate_up_ref[index].astype(jnp.float32).reshape(blocks, height, -1)
        scaled = values * gate_up_scale_ref[0, index][:, None, :]
        return scaled.reshape(features, -1).astype(jnp.bfloat16)

    both = jnp.concatenate([projection(0), projection(1)], axis=1)
    act = jnp.dot(rows_ref[...], both, preferred_element_type=jnp.float32)
    width = act.shape[1] // 2
    gate_act, up_act = act[:, :width], act[:, width:]
    inner = (gate_act / (1.0 + jnp.exp(-gate_act)) * up_act).astype(jnp.bfloat16)
    down = (down_ref[...].astype(jnp.float32) * down_scale_ref[0]).astype(jnp.bfloat16)
    term = jnp.dot(inner, down, preferred_element_type=jnp.float32)

    @pl.when(step == 0)
    def _():
        total[...] = term

    @pl.when(step > 0)
    def _():
        total[...] += term

    @pl.when(step == pl.num_programs(0) - 1)
    def _():
        out_ref[...] = (total[...] * share_ref[...]).astype(out_ref.dtype)


def expert_partial(rows, shares, gate_up, gate_up_scales, down, down_scales):
    count, features = rows.shape
    hidden_units = down.shape[0]
    blocks = down_scales.shape[0]
    width = hidden_units // blocks
    tall = gate_up_scales.shape[1]
    chunk = min(count, 512)
    gate_up_scale = jnp.broadcast_to(
        gate_up_scales.astype(jnp.float32).transpose(2, 0, 1)[..., None], (blocks, 2, tall, width)
    )
    down_scale = jnp.repeat(down_scales.astype(jnp.float32), features // down_scales.shape[1], axis=1)
    down_scale = down_scale[:, None, :]

    def call(piece, share):
        return pl.pallas_call(
            expert_kernel,
            grid=(blocks,),
            out_shape=jax.ShapeDtypeStruct((chunk, features), jnp.bfloat16),
            in_specs=[
                pl.BlockSpec((chunk, features), lambda j: (0, 0)),
                pl.BlockSpec((2, features, width), lambda j: (0, 0, j)),
                pl.BlockSpec((1, 2, tall, width), lambda j: (j, 0, 0, 0)),
                pl.BlockSpec((width, features), lambda j: (j, 0)),
                pl.BlockSpec((1, 1, features), lambda j: (j, 0, 0)),
                pl.BlockSpec((chunk, 1), lambda j: (0, 0)),
            ],
            out_specs=pl.BlockSpec((chunk, features), lambda j: (0, 0)),
            scratch_shapes=[pltpu.VMEM((chunk, features), jnp.float32)],
            compiler_params=pltpu.CompilerParams(vmem_limit_bytes=56 * 1024 * 1024),
            cost_estimate=pl.CostEstimate(
                flops=6 * chunk * features * hidden_units,
                bytes_accessed=6 * features * hidden_units + 4 * chunk * features,
                transcendentals=chunk * hidden_units,
            ),
        )(piece, gate_up, gate_up_scale, down, down_scale, share)

    if count == chunk:
        return call(rows, shares)
    pieces = lax.map(
        lambda pair: call(*pair),
        (rows.reshape(-1, chunk, features), shares.reshape(-1, chunk, 1)),
    )
    return pieces.reshape(count, features)


def halved(terms, axis, bit, index):
    mine = (index >> bit) & 1
    kept = lax.dynamic_index_in_dim(terms, mine, 0, keepdims=False)
    sent = lax.dynamic_index_in_dim(terms, 1 - mine, 0, keepdims=False)
    got = partner(sent, axis, bit)
    return (kept.astype(jnp.float32) + got.astype(jnp.float32)).astype(jnp.bfloat16)


def summed_home(terms, experts, copies):
    rest = terms.shape[1:]
    my_expert, my_copy = lax.axis_index("expert"), lax.axis_index("replica")
    expert_bits, copy_bits = experts.bit_length() - 1, copies.bit_length() - 1
    shape = [2] * (expert_bits + copy_bits)
    names = [("e", bit) for bit in reversed(range(expert_bits))] + [
        ("c", bit) for bit in reversed(range(copy_bits))
    ]
    order = [("e", 0)] + [("c", b) for b in range(copy_bits)] + [("e", b) for b in range(1, expert_bits)]
    terms = terms.reshape(shape + list(rest))
    terms = terms.transpose([names.index(o) for o in order] + [len(names), len(names) + 1])
    for kind, bit in order:
        axis, index = ("expert", my_expert) if kind == "e" else ("replica", my_copy)
        terms = halved(terms, axis, bit, index)
    return terms


def body(
    hidden_first,
    hidden_second,
    routes_first,
    routes_second,
    mixing_first,
    mixing_second,
    norm_gain,
    expert_owner,
    swap_flags,
    gate_up_values,
    gate_up_scales,
    down_values,
    down_scales,
):
    experts = lax.axis_size("expert")
    copies = lax.axis_size("replica")
    my_slot = lax.axis_index("expert")
    tokens_here, features = hidden_first.shape
    slot_ids = jnp.arange(experts, dtype=jnp.int32)

    hidden = jnp.concatenate([hidden_first, hidden_second], axis=0)
    routes = jnp.concatenate([routes_first, routes_second], axis=0)
    mixing = jnp.concatenate([mixing_first, mixing_second], axis=0)
    normed = rms_normed(hidden, norm_gain)
    shares = jnp.sum(
        jnp.where(routes[:, :, None] == slot_ids, mixing[:, :, None], 0.0), axis=1
    )
    all_rows = lax.all_gather(normed, ("expert", "replica"), axis=0, tiled=True)
    all_shares = lax.all_gather(shares, ("expert", "replica"), axis=0, tiled=True)
    mine = expert_owner == my_slot
    my_shares = jnp.sum(jnp.where(mine[None, :], all_shares, 0.0), axis=1, keepdims=True)
    terms = expert_partial(
        all_rows, my_shares, gate_up_values[0], gate_up_scales[0], down_values[0], down_scales[0]
    )
    merged = summed_home(
        terms.reshape(experts * copies, 2 * tokens_here, features), experts, copies
    )

    flagged = jnp.sum(jnp.where(slot_ids == my_slot, swap_flags, 0)) == 1
    current = (gate_up_values, gate_up_scales, down_values, down_scales)
    current, merged = lax.optimization_barrier((current, merged))
    moved = lax.cond(
        flagged,
        lambda pieces: partner(pieces, "expert", experts.bit_length() - 2),
        lambda pieces: pieces,
        current,
    )
    return (merged[:tokens_here], merged[tokens_here:]) + tuple(moved)


def solution(mesh):
    rows = P(("expert", "replica"), None)
    weights = (
        P("expert", None, None, "replica"),
        P("expert", None, None, "replica"),
        P("expert", "replica", None),
        P("expert", "replica", None),
    )
    return jax.shard_map(
        body,
        mesh=mesh,
        in_specs=(rows,) * 6 + (P(),) * 3 + weights,
        out_specs=(rows, rows) + weights,
        check_vma=False,
    )
```

```python
import functools

import jax
import jax.numpy as jnp
from jax import lax
from jax.experimental import pallas as pl
from jax.experimental.pallas import tpu as pltpu
from jax.sharding import PartitionSpec as P

LANES = 128


def partner(block, axis, bit):
    count = lax.axis_size(axis)
    route = [(low, low ^ (1 << bit)) for low in range(count)]
    return lax.ppermute(block, axis, route)


def rms_normed(hidden, norm_gain):
    widened = hidden.astype(jnp.float32)
    inverse_rms = lax.rsqrt(jnp.mean(widened * widened, axis=-1, keepdims=True) + 1e-06)
    return (widened * inverse_rms * norm_gain).astype(jnp.bfloat16)


def expert_kernel(rows_ref, gate_up_ref, gate_up_scale_ref, down_ref, down_scale_ref, share_ref, out_ref, total):
    step = pl.program_id(1)
    features = rows_ref.shape[1]
    blocks = gate_up_scale_ref.shape[2]
    height = features // blocks

    def projection(index):
        values = gate_up_ref[index].astype(jnp.float32).reshape(blocks, height, -1)
        scaled = values * gate_up_scale_ref[0, index][:, None, :]
        return scaled.reshape(features, -1).astype(jnp.bfloat16)

    both = jnp.concatenate([projection(0), projection(1)], axis=1)
    act = jnp.dot(rows_ref[...], both, preferred_element_type=jnp.float32)
    width = act.shape[1] // 2
    gate_act, up_act = act[:, :width], act[:, width:]
    inner = (gate_act / (1.0 + jnp.exp(-gate_act)) * up_act).astype(jnp.bfloat16)
    down = (down_ref[...].astype(jnp.float32) * down_scale_ref[0]).astype(jnp.bfloat16)
    term = jnp.dot(inner, down, preferred_element_type=jnp.float32)

    @pl.when(step == 0)
    def _():
        total[...] = term

    @pl.when(step > 0)
    def _():
        total[...] += term

    @pl.when(step == pl.num_programs(1) - 1)
    def _():
        out_ref[...] = (total[...] * share_ref[...]).astype(out_ref.dtype)


def expert_partial(rows, features, shares, gate_up, gate_up_scales, down, down_scales):
    count = rows.shape[0]
    hidden_units = down.shape[0]
    blocks = down_scales.shape[0]
    width = hidden_units // blocks
    tall = gate_up_scales.shape[1]
    chunk = min(count, 512)
    gate_up_scale = jnp.broadcast_to(
        gate_up_scales.astype(jnp.float32).transpose(2, 0, 1)[..., None], (blocks, 2, tall, width)
    )
    down_scale = jnp.repeat(down_scales.astype(jnp.float32), features // down_scales.shape[1], axis=1)
    down_scale = down_scale[:, None, :]

    return pl.pallas_call(
        expert_kernel,
        grid=(count // chunk, blocks),
        out_shape=jax.ShapeDtypeStruct((count, features), jnp.bfloat16),
        in_specs=[
            pl.BlockSpec((chunk, features), lambda c, j: (c, 0)),
            pl.BlockSpec((2, features, width), lambda c, j: (0, 0, j)),
            pl.BlockSpec((1, 2, tall, width), lambda c, j: (j, 0, 0, 0)),
            pl.BlockSpec((width, features), lambda c, j: (j, 0)),
            pl.BlockSpec((1, 1, features), lambda c, j: (j, 0, 0)),
            pl.BlockSpec((chunk, 1), lambda c, j: (c, 0)),
        ],
        out_specs=pl.BlockSpec((chunk, features), lambda c, j: (c, 0)),
        scratch_shapes=[pltpu.VMEM((chunk, features), jnp.float32)],
        compiler_params=pltpu.CompilerParams(vmem_limit_bytes=56 * 1024 * 1024),
        cost_estimate=pl.CostEstimate(
            flops=6 * count * features * hidden_units,
            bytes_accessed=6 * features * hidden_units + 4 * count * features,
            transcendentals=count * hidden_units,
        ),
    )(rows, gate_up, gate_up_scale, down, down_scale, shares)


def halved(terms, axis, bit, index):
    mine = (index >> bit) & 1
    kept = lax.dynamic_index_in_dim(terms, mine, 0, keepdims=False)
    sent = lax.dynamic_index_in_dim(terms, 1 - mine, 0, keepdims=False)
    got = partner(sent, axis, bit)
    return (kept.astype(jnp.float32) + got.astype(jnp.float32)).astype(jnp.bfloat16)


def summed_home(terms, experts, copies):
    rest = terms.shape[1:]
    my_expert, my_copy = lax.axis_index("expert"), lax.axis_index("replica")
    expert_bits, copy_bits = experts.bit_length() - 1, copies.bit_length() - 1
    shape = [2] * (expert_bits + copy_bits)
    names = [("e", bit) for bit in reversed(range(expert_bits))] + [
        ("c", bit) for bit in reversed(range(copy_bits))
    ]
    order = [("e", 0)] + [("c", b) for b in range(copy_bits)] + [("e", b) for b in range(1, expert_bits)]
    terms = terms.reshape(shape + list(rest))
    terms = terms.transpose([names.index(o) for o in order] + [len(names), len(names) + 1])
    for kind, bit in order:
        axis, index = ("expert", my_expert) if kind == "e" else ("replica", my_copy)
        terms = halved(terms, axis, bit, index)
    return terms


def body(
    hidden_first,
    hidden_second,
    routes_first,
    routes_second,
    mixing_first,
    mixing_second,
    norm_gain,
    expert_owner,
    swap_flags,
    gate_up_values,
    gate_up_scales,
    down_values,
    down_scales,
):
    experts = lax.axis_size("expert")
    copies = lax.axis_size("replica")
    my_slot = lax.axis_index("expert")
    tokens_here, features = hidden_first.shape
    slot_ids = jnp.arange(experts, dtype=jnp.int32)

    hidden = jnp.concatenate([hidden_first, hidden_second], axis=0)
    routes = jnp.concatenate([routes_first, routes_second], axis=0)
    mixing = jnp.concatenate([mixing_first, mixing_second], axis=0)
    normed = rms_normed(hidden, norm_gain)
    shares = jnp.sum(
        jnp.where(routes[:, :, None] == slot_ids, mixing[:, :, None], 0.0), axis=1
    )
    upper = lax.reduce_precision(shares, 8, 7)
    pieces = jnp.concatenate([upper, shares - upper], axis=1).astype(jnp.bfloat16)
    extra = -(-2 * experts // LANES) * LANES
    pieces = jnp.pad(pieces, ((0, 0), (0, extra - 2 * experts)))
    sent_rows, swap_flags = lax.optimization_barrier(
        (jnp.concatenate([normed, pieces], axis=1), swap_flags)
    )
    all_rows = lax.all_gather(sent_rows, ("expert", "replica"), axis=0, tiled=True)

    flagged = jnp.sum(jnp.where(slot_ids == my_slot, swap_flags, 0)) == 1
    half_bit = experts.bit_length() - 2
    gate_up_moved = lax.cond(
        flagged,
        lambda given: partner(given, "expert", half_bit),
        lambda given: given,
        (gate_up_values, gate_up_scales),
    )
    all_rows, gate_up_moved = lax.optimization_barrier((all_rows, gate_up_moved))
    mine = expert_owner == my_slot
    both = all_rows[:, features : features + 2 * experts].astype(jnp.float32)
    all_shares = both[:, :experts] + both[:, experts:]
    my_shares = jnp.sum(jnp.where(mine[None, :], all_shares, 0.0), axis=1, keepdims=True)

    def computed(given):
        return expert_partial(
            all_rows, features, my_shares, gate_up_values[0], gate_up_scales[0], given[0][0], given[1][0]
        )

    down_moved, terms = lax.cond(
        flagged,
        lambda given: (partner(given, "expert", half_bit), computed(given)),
        lambda given: (given, computed(given)),
        (down_values, down_scales),
    )
    merged = summed_home(
        terms.reshape(experts * copies, 2 * tokens_here, features), experts, copies
    )
    moved = gate_up_moved + down_moved
    return (merged[:tokens_here], merged[tokens_here:]) + tuple(moved)


def solution(mesh):
    rows = P(("expert", "replica"), None)
    weights = (
        P("expert", None, None, "replica"),
        P("expert", None, None, "replica"),
        P("expert", "replica", None),
        P("expert", "replica", None),
    )
    return jax.shard_map(
        body,
        mesh=mesh,
        in_specs=(rows,) * 6 + (P(),) * 3 + weights,
        out_specs=(rows, rows) + weights,
        check_vma=False,
    )
```

```python
import functools

import jax
import jax.numpy as jnp
from jax import lax
from jax.experimental import pallas as pl
from jax.experimental.pallas import tpu as pltpu
from jax.sharding import PartitionSpec as P

LANES = 128


def partner(block, axis, bit):
    count = lax.axis_size(axis)
    route = [(low, low ^ (1 << bit)) for low in range(count)]
    return lax.ppermute(block, axis, route)


def rms_normed(hidden, norm_gain):
    widened = hidden.astype(jnp.float32)
    inverse_rms = lax.rsqrt(jnp.mean(widened * widened, axis=-1, keepdims=True) + 1e-06)
    return (widened * inverse_rms * norm_gain).astype(jnp.bfloat16)


def expert_kernel(rows_ref, gate_up_ref, gate_up_scale_ref, down_ref, down_scale_ref, share_ref, out_ref, total):
    step = pl.program_id(1)
    features = rows_ref.shape[1]
    blocks = gate_up_scale_ref.shape[2]
    height = features // blocks

    def projection(index):
        values = gate_up_ref[index].astype(jnp.float32).reshape(blocks, height, -1)
        scaled = values * gate_up_scale_ref[0, index][:, None, :]
        return scaled.reshape(features, -1).astype(jnp.bfloat16)

    both = jnp.concatenate([projection(0), projection(1)], axis=1)
    act = jnp.dot(rows_ref[...], both, preferred_element_type=jnp.float32)
    width = act.shape[1] // 2
    gate_act, up_act = act[:, :width], act[:, width:]
    inner = (gate_act / (1.0 + jnp.exp(-gate_act)) * up_act).astype(jnp.bfloat16)
    down = (down_ref[...].astype(jnp.float32) * down_scale_ref[0]).astype(jnp.bfloat16)
    term = jnp.dot(inner, down, preferred_element_type=jnp.float32)

    @pl.when(step == 0)
    def _():
        total[...] = term

    @pl.when(step > 0)
    def _():
        total[...] += term

    @pl.when(step == pl.num_programs(1) - 1)
    def _():
        out_ref[...] = (total[...] * share_ref[...]).astype(out_ref.dtype)


def expert_partial(rows, features, shares, gate_up, gate_up_scales, down, down_scales):
    count = rows.shape[0]
    hidden_units = down.shape[0]
    blocks = down_scales.shape[0]
    width = hidden_units // blocks
    tall = gate_up_scales.shape[1]
    chunk = min(count, 512)
    gate_up_scale = jnp.broadcast_to(
        gate_up_scales.astype(jnp.float32).transpose(2, 0, 1)[..., None], (blocks, 2, tall, width)
    )
    down_scale = jnp.repeat(down_scales.astype(jnp.float32), features // down_scales.shape[1], axis=1)
    down_scale = down_scale[:, None, :]

    return pl.pallas_call(
        expert_kernel,
        grid=(count // chunk, blocks),
        out_shape=jax.ShapeDtypeStruct((count, features), jnp.bfloat16),
        in_specs=[
            pl.BlockSpec((chunk, features), lambda c, j: (c, 0)),
            pl.BlockSpec((2, features, width), lambda c, j: (0, 0, j)),
            pl.BlockSpec((1, 2, tall, width), lambda c, j: (j, 0, 0, 0)),
            pl.BlockSpec((width, features), lambda c, j: (j, 0)),
            pl.BlockSpec((1, 1, features), lambda c, j: (j, 0, 0)),
            pl.BlockSpec((chunk, 1), lambda c, j: (c, 0)),
        ],
        out_specs=pl.BlockSpec((chunk, features), lambda c, j: (c, 0)),
        scratch_shapes=[pltpu.VMEM((chunk, features), jnp.float32)],
        compiler_params=pltpu.CompilerParams(vmem_limit_bytes=56 * 1024 * 1024),
        cost_estimate=pl.CostEstimate(
            flops=6 * count * features * hidden_units,
            bytes_accessed=6 * features * hidden_units + 4 * count * features,
            transcendentals=count * hidden_units,
        ),
    )(rows, gate_up, gate_up_scale, down, down_scale, shares)


def halved(terms, dim, axis, bit):
    mine = (lax.axis_index(axis) >> bit) & 1
    kept = lax.dynamic_index_in_dim(terms, mine, dim, keepdims=False)
    sent = lax.dynamic_index_in_dim(terms, 1 - mine, dim, keepdims=False)
    got = partner(sent, axis, bit)
    return (kept.astype(jnp.float32) + got.astype(jnp.float32)).astype(jnp.bfloat16)


def summed_home(terms, experts, copies):
    rest = list(terms.shape[1:])
    expert_bits, copy_bits = experts.bit_length() - 1, copies.bit_length() - 1
    names = [("expert", bit) for bit in reversed(range(expert_bits))] + [
        ("replica", bit) for bit in reversed(range(copy_bits))
    ]
    first, second, third = ("expert", 0), ("replica", 0), ("expert", 1)
    order = [first, second, third] + sorted(
        (name for name in names if name not in (first, second, third)), key=lambda name: name[1]
    )
    terms = terms.reshape([2] * len(names) + rest)
    terms = terms.transpose([names.index(o) for o in order] + [len(names), len(names) + 1])
    terms = halved(terms, 0, *first)
    middle = rest[1] // 2
    left, right = terms[..., :middle], terms[..., middle:]
    left, right = halved(left, 0, *second), halved(right, 1, *third)
    left, right = halved(left, 0, *third), halved(right, 0, *second)
    terms = jnp.concatenate([left, right], axis=-1)
    for axis, bit in order[3:]:
        terms = halved(terms, 0, axis, bit)
    return terms


def body(
    hidden_first,
    hidden_second,
    routes_first,
    routes_second,
    mixing_first,
    mixing_second,
    norm_gain,
    expert_owner,
    swap_flags,
    gate_up_values,
    gate_up_scales,
    down_values,
    down_scales,
):
    experts = lax.axis_size("expert")
    copies = lax.axis_size("replica")
    my_slot = lax.axis_index("expert")
    tokens_here, features = hidden_first.shape
    slot_ids = jnp.arange(experts, dtype=jnp.int32)

    hidden = jnp.concatenate([hidden_first, hidden_second], axis=0)
    routes = jnp.concatenate([routes_first, routes_second], axis=0)
    mixing = jnp.concatenate([mixing_first, mixing_second], axis=0)
    normed = rms_normed(hidden, norm_gain)
    shares = jnp.sum(
        jnp.where(routes[:, :, None] == slot_ids, mixing[:, :, None], 0.0), axis=1
    )
    upper = lax.reduce_precision(shares, 8, 7)
    pieces = jnp.concatenate([upper, shares - upper], axis=1).astype(jnp.bfloat16)
    extra = -(-2 * experts // LANES) * LANES
    pieces = jnp.pad(pieces, ((0, 0), (0, extra - 2 * experts)))
    sent_rows, swap_flags = lax.optimization_barrier(
        (jnp.concatenate([normed, pieces], axis=1), swap_flags)
    )
    all_rows = lax.all_gather(sent_rows, ("expert", "replica"), axis=0, tiled=True)

    flagged = jnp.sum(jnp.where(slot_ids == my_slot, swap_flags, 0)) == 1
    half_bit = experts.bit_length() - 2
    gate_up_moved = lax.cond(
        flagged,
        lambda given: partner(given, "expert", half_bit),
        lambda given: given,
        (gate_up_values, gate_up_scales),
    )
    all_rows, scales_moved = lax.optimization_barrier((all_rows, gate_up_moved[1]))
    mine = expert_owner == my_slot
    both = all_rows[:, features : features + 2 * experts].astype(jnp.float32)
    all_shares = both[:, :experts] + both[:, experts:]
    my_shares = jnp.sum(jnp.where(mine[None, :], all_shares, 0.0), axis=1, keepdims=True)

    def computed(given):
        return expert_partial(
            all_rows, features, my_shares, gate_up_values[0], gate_up_scales[0], given[0][0], given[1][0]
        )

    down_moved, terms = lax.cond(
        flagged,
        lambda given: (partner(given, "expert", half_bit), computed(given)),
        lambda given: (given, computed(given)),
        (down_values, down_scales),
    )
    merged = summed_home(
        terms.reshape(experts * copies, 2 * tokens_here, features), experts, copies
    )
    moved = (gate_up_moved[0], scales_moved) + tuple(down_moved)
    return (merged[:tokens_here], merged[tokens_here:]) + tuple(moved)


def solution(mesh):
    rows = P(("expert", "replica"), None)
    weights = (
        P("expert", None, None, "replica"),
        P("expert", None, None, "replica"),
        P("expert", "replica", None),
        P("expert", "replica", None),
    )
    return jax.shard_map(
        body,
        mesh=mesh,
        in_specs=(rows,) * 6 + (P(),) * 3 + weights,
        out_specs=(rows, rows) + weights,
        check_vma=False,
    )
```
